512 devices in a mesh: hi: 4 (over z_hi, core), lo: 128 (over y, z_lo, x).
Axes of the slice: x: 4, y: 4, z: 16 (z_hi: 2, z_lo: 8; z = z_hi * 8 + z_lo), core: 2. Of those that a mesh axis runs over, the one named last changes fastest.
Arguments:
- state: float32 [2, 2048, 128, 128], P(None, ('hi', 'lo')), may hold values from -6 to 6
- low_gates: float32 [2, 2, 128, 128], replicated, may hold values from -0.375 to 0.375
- low_order: int32 [2, 7], replicated, may hold values from 0 to 6, each once within a row
- high_gates: float32 [2, 2, 2, 2], replicated, may hold values from -3 to 3
- mid_gate: float32 [2, 128, 128], replicated, may hold values from -0.375 to 0.375
- mid_order: int32 [7], replicated, may hold values from 0 to 6, each once
Outputs:
- final_state: float32 [2, 2048, 128, 128], P(None, ('hi', 'lo'))
The draws below stay inside these ranges and needn't reach their ends.
Inputs may be any that keep to these rules, and one draw needn't show every extreme that they name: `low_order`: each row is an order of the 7 low qubits, each once. `mid_order`: an order of the 7 qubits, each once.
All inputs are finite; a program needn't handle non-finite values.
Results may differ from the reference program's by a relative error of at most 0.000082.
Values sent between devices are 32-bit elements; how exact they have to be, the bound alone decides.
No kernel may reach another device: no remote copies, remote signals or barrier semaphores. Data moves between devices by JAX's collectives and lax.ppermute only.
A program may use at most 64 MiB of HBM per device.

```python
import jax
import jax.numpy as jnp
from jax import lax

LOW_QUBITS = 7
MID_QUBITS = 7
LOW = 128
GATE = 128
SUB = 4
ROWS = 2048
N_HI = 4
N_LO = 128


def level_of(own_key, dims, pieces, low, largest):
    def one(axis_at, blocks):
        steps = jax.random.uniform(jax.random.fold_in(jax.random.fold_in(own_key, 6), axis_at), (blocks,), jnp.float32, low / len(pieces), largest / len(pieces))
        return jnp.repeat(jnp.exp(steps), dims[axis_at] // blocks).reshape((-1,) + (1,) * (len(dims) - axis_at - 1))

    loudness = one(*pieces[0])
    for cut in pieces[1:]:
        loudness = loudness * one(*cut)
    return loudness


def gaussian(key, dims, width, limit, cuts=(), held_as=jnp.bfloat16):
    gain = level_of(key, dims, cuts, -0.22, 0.18) if cuts else 1.0
    array = jax.random.normal(key, dims, jnp.float32) * width * gain
    return jnp.minimum(jnp.maximum(array, -limit), limit).astype(held_as)


def setup_inputs(seed: int = 0) -> dict:
    key_list = jax.random.split(jax.random.key(seed), 7)
    state = gaussian(key_list[0], (2, ROWS, GATE, LOW), 1.0, 6.0, ((1, 512),), jnp.float32)
    low_gates = gaussian(key_list[1], (2, 2, LOW, LOW), (2 * LOW) ** -0.5, 0.375, (), jnp.float32)
    low_order = jax.vmap(lambda own: jax.random.permutation(own, LOW_QUBITS))(jax.random.split(key_list[2], 2)).reshape((2, LOW_QUBITS)).astype(jnp.int32)
    high_gates = gaussian(key_list[3], (2, 2, 2, 2), 4 ** -0.5, 3.0, (), jnp.float32)
    mid_gate = gaussian(key_list[4], (2, GATE, GATE), (2 * GATE) ** -0.5, 0.375, (), jnp.float32)
    mid_order = jax.random.permutation(key_list[5], MID_QUBITS).astype(jnp.int32)
    return {"state": state, "low_gates": low_gates, "low_order": low_order, "high_gates": high_gates, "mid_gate": mid_gate, "mid_order": mid_order}


def index_map(order):
    count = order.shape[0]
    values = jnp.arange(2 ** count, dtype=jnp.int32)
    places = jnp.arange(count, dtype=jnp.int32)
    bits = (values[:, None] >> places[None, :]) & 1
    return jnp.sum(bits << order[None, :].astype(jnp.int32), axis=1).astype(jnp.int32)


def permuted(gate, order):
    where = index_map(order)
    return gate[:, where][:, :, where]


def apply_last(real, imag, matrix):
    def prod(left, right):
        return jnp.einsum("...b,ab->...a", left, right, precision=lax.Precision.HIGHEST)
    return prod(real, matrix[0]) - prod(imag, matrix[1]), prod(real, matrix[1]) + prod(imag, matrix[0])


def combine(self_re, self_im, other_re, other_im, coef_self, coef_other):
    real = (coef_self[0] * self_re - coef_self[1] * self_im) + (coef_other[0] * other_re - coef_other[1] * other_im)
    imag = (coef_self[0] * self_im + coef_self[1] * self_re) + (coef_other[0] * other_im + coef_other[1] * other_re)
    return jnp.stack([real, imag])


def high_local(grouped, high_gates):
    for qubit in range(2):
        axis = 2 - qubit
        halves = []
        for level in range(2):
            mine = jnp.take(grouped, level, axis=axis)
            other = jnp.take(grouped, 1 - level, axis=axis)
            unit = high_gates[qubit]
            halves.append(combine(mine[0], mine[1], other[0], other[1], unit[:, level, level], unit[:, level, 1 - level]))
        grouped = jnp.stack(halves, axis=axis)
    return grouped


def reference(state, low_gates, low_order, high_gates, mid_gate, mid_order):
    first_matrix = permuted(low_gates[0], low_order[0])
    second_matrix = permuted(low_gates[1], low_order[1])
    mid_matrix = permuted(mid_gate, mid_order)
    real, imag = apply_last(state[0], state[1], first_matrix)
    first = jnp.stack([real, imag])
    grouped = first.reshape(2, 2, 2, N_LO * SUB, GATE, LOW)
    second = high_local(grouped, high_gates).reshape(2, ROWS, GATE, LOW)
    split = second.reshape(2, N_HI, N_LO, SUB, N_LO, GATE // N_LO, LOW)
    moved = jnp.transpose(split, (0, 1, 3, 4, 6, 2, 5)).reshape(2, N_HI, SUB, N_LO, LOW, GATE)
    real, imag = apply_last(moved[0], moved[1], mid_matrix)
    third = jnp.stack([real, imag]).reshape(2, N_HI, SUB, N_LO, LOW, N_LO, GATE // N_LO)
    third = jnp.transpose(third, (0, 1, 5, 2, 3, 6, 4)).reshape(2, ROWS, GATE, LOW)
    real, imag = apply_last(third[0], third[1], second_matrix)
    return jnp.stack([real, imag])
```

```python
import jax
import jax.numpy as jnp
from jax import lax
from jax.sharding import PartitionSpec as P

AXES = ("hi", "lo")
HIGHEST = lax.Precision.HIGHEST


def index_map(order):
    count = order.shape[0]
    values = jnp.arange(2**count, dtype=jnp.int32)
    places = jnp.arange(count, dtype=jnp.int32)
    bits = values[:, None] >> places[None, :] & 1
    return jnp.sum(bits << order[None, :], axis=1)


def permuted(gate, order):
    where = index_map(order)
    pick = (where[:, None] == jnp.arange(gate.shape[-1])[None, :]).astype(gate.dtype)
    half = jnp.einsum("ai,cij->caj", pick, gate, precision=HIGHEST)
    return jnp.einsum("caj,bj->cab", half, pick, precision=HIGHEST)


def product(left, right):
    def prod(a, b):
        return jnp.dot(a, b, precision=HIGHEST)

    return jnp.stack(
        [
            prod(left[0], right[0]) - prod(left[1], right[1]),
            prod(left[0], right[1]) + prod(left[1], right[0]),
        ]
    )


def combine(mine, other, unit, level):
    own, cross = unit[:, level, level], unit[:, level, 1 - level]
    return (
        own[0] * mine[0] - own[1] * mine[1] + (cross[0] * other[0] - cross[1] * other[1]),
        own[0] * mine[1] + own[1] * mine[0] + (cross[0] * other[1] + cross[1] * other[0]),
    )


def high(parts, high_gates):
    for qubit in range(2):
        parts = [
            combine(parts[h], parts[h ^ 1 << qubit], high_gates[qubit], h >> qubit & 1)
            for h in range(4)
        ]
    return parts


def body(state, low_gates, low_order, high_gates, mid_gate, mid_order):
    rows, order = state.shape[1], state.shape[3]
    peers = rows * state.shape[2]
    low = product(permuted(low_gates[1], low_order[1]), permuted(low_gates[0], low_order[0]))
    mid = permuted(mid_gate, mid_order)
    sent = jnp.transpose(state, (1, 2, 0, 3)).reshape(peers, 2, order)
    moved = lax.all_to_all(sent, AXES, 0, 0, tiled=True)
    group = moved.reshape(4, -1, 2, order)
    parts = high([(group[h, :, 0], group[h, :, 1]) for h in range(4)], high_gates)
    stacked = jnp.concatenate(
        [jnp.concatenate([re, im], axis=0) for re, im in parts], axis=1
    )
    mid_real = jnp.concatenate(
        [jnp.concatenate([mid[0], -mid[1]], 1), jnp.concatenate([mid[1], mid[0]], 1)], 0
    )
    mixed = jnp.dot(mid_real, stacked, precision=lax.Precision.HIGH)
    size = mid.shape[1]
    mixed = mixed.reshape(2, size, 4, order).transpose(2, 1, 0, 3).reshape(peers, 2 * order)
    low_real = jnp.concatenate(
        [jnp.concatenate([low[0].T, low[1].T], 1), jnp.concatenate([-low[1].T, low[0].T], 1)], 0
    )
    last = jnp.dot(mixed, low_real, precision=lax.Precision.HIGH)
    back = lax.all_to_all(last.reshape(peers, 2, order), AXES, 0, 0, tiled=True)
    return jnp.transpose(back.reshape(rows, -1, 2, order), (2, 0, 1, 3))


def solution(mesh):
    return jax.shard_map(
        body,
        mesh=mesh,
        in_specs=(P(None, AXES, None, None), P(), P(), P(), P(), P()),
        out_specs=P(None, AXES, None, None),
        check_vma=False,
    )
```

```python
import jax
import jax.numpy as jnp
from jax import lax
from jax.experimental import pallas as pl
from jax.experimental.pallas import tpu as pltpu
from jax.sharding import PartitionSpec as P

AXES = ("hi", "lo")
HIGHEST = lax.Precision.HIGHEST
IN_VMEM = pl.BlockSpec(memory_space=pltpu.VMEM)


def index_map(order):
    count = order.shape[0]
    values = jnp.arange(2**count, dtype=jnp.int32)
    places = jnp.arange(count, dtype=jnp.int32)
    bits = values[:, None] >> places[None, :] & 1
    return jnp.sum(bits << order[None, :], axis=1)


def permuted(gate, order):
    where = index_map(order)
    pick = (where[:, None] == jnp.arange(gate.shape[-1])[None, :]).astype(gate.dtype)
    half = jnp.einsum("ai,cij->caj", pick, gate, precision=HIGHEST)
    return jnp.einsum("caj,bj->cab", half, pick, precision=HIGHEST)


def product(left, right):
    def prod(a, b):
        return jnp.dot(a, b, precision=HIGHEST)

    return jnp.stack(
        [
            prod(left[0], right[0]) - prod(left[1], right[1]),
            prod(left[0], right[1]) + prod(left[1], right[0]),
        ]
    )


def as_real(matrix):
    return jnp.concatenate(
        [
            jnp.concatenate([matrix[0], -matrix[1]], axis=1),
            jnp.concatenate([matrix[1], matrix[0]], axis=1),
        ],
        axis=0,
    )


def split(value):
    top = value.astype(jnp.bfloat16)
    return top, (value - top.astype(jnp.float32)).astype(jnp.bfloat16)


def dot3(left, right):
    def prod(a, b):
        return jnp.dot(a, b, preferred_element_type=jnp.float32)

    (left_top, left_rest), (right_top, right_rest) = split(left), split(right)
    return prod(left_top, right_rest) + prod(left_rest, right_top) + prod(left_top, right_top)


def combine(mine, other, own, cross):
    return (
        own[0] * mine[0] - own[1] * mine[1] + (cross[0] * other[0] - cross[1] * other[1]),
        own[0] * mine[1] + own[1] * mine[0] + (cross[0] * other[1] + cross[1] * other[0]),
    )


def middle_kernel(moved_ref, units_ref, mid_ref, low_ref, out_ref):
    rows, order = moved_ref.shape
    size = rows // 8

    def unit(qubit, into, source):
        at = qubit * 8 + into * 2 + source
        return units_ref[at : at + 1, :], units_ref[at + 4 : at + 5, :]

    parts = [
        tuple(moved_ref[pl.ds(h * size * 2 + c, size, 2), :] for c in range(2)) for h in range(4)
    ]
    for qubit in range(2):
        levels = [h >> qubit & 1 for h in range(4)]
        parts = [
            combine(
                parts[h],
                parts[h ^ 1 << qubit],
                unit(qubit, levels[h], levels[h]),
                unit(qubit, levels[h], 1 - levels[h]),
            )
            for h in range(4)
        ]
    stacked = jnp.concatenate([jnp.concatenate([re, im], axis=0) for re, im in parts], axis=1)
    mixed = dot3(mid_ref[...], stacked)
    turned = jnp.concatenate(
        [
            jnp.concatenate(
                [
                    mixed[c * size : (c + 1) * size, h * order : (h + 1) * order]
                    for c in range(2)
                ],
                axis=1,
            )
            for h in range(4)
        ],
        axis=0,
    )
    last = dot3(turned, low_ref[...])
    for c in range(2):
        out_ref[pl.ds(c, rows // 2, 2), :] = last[:, c * order : (c + 1) * order]


def interleave_kernel(state_ref, out_ref):
    half = state_ref.shape[1]
    for c in range(2):
        out_ref[pl.ds(c, half, 2), :] = state_ref[c]


def separate_kernel(rows_ref, out_ref):
    half = out_ref.shape[1]
    for c in range(2):
        out_ref[c] = rows_ref[pl.ds(c, half, 2), :]


def call(kernel, shape, *operands):
    return pl.pallas_call(
        kernel,
        out_shape=jax.ShapeDtypeStruct(shape, jnp.float32),
        in_specs=[IN_VMEM] * len(operands),
        out_specs=IN_VMEM,
        compiler_params=pltpu.CompilerParams(vmem_limit_bytes=32 * 2**20),
    )(*operands)


def exchange(rows, peers):
    moved = lax.all_to_all(rows.reshape(peers, 2, -1), AXES, 0, 0, tiled=True)
    return moved.reshape(rows.shape)


def body(state, low_gates, low_order, high_gates, mid_gate, mid_order):
    order = state.shape[3]
    peers = state.shape[1] * state.shape[2]
    low = product(permuted(low_gates[1], low_order[1]), permuted(low_gates[0], low_order[0]))
    mid = permuted(mid_gate, mid_order)
    units = jnp.broadcast_to(high_gates.reshape(16, 1), (16, order))
    sent = call(interleave_kernel, (2 * peers, order), state.reshape(2, peers, order))
    moved = exchange(sent, peers)
    done = call(middle_kernel, moved.shape, moved, units, as_real(mid), as_real(low).T)
    back = exchange(done, peers)
    return call(separate_kernel, (2, peers, order), back).reshape(state.shape)


def solution(mesh):
    return jax.shard_map(
        body,
        mesh=mesh,
        in_specs=(P(None, AXES, None, None), P(), P(), P(), P(), P()),
        out_specs=P(None, AXES, None, None),
        check_vma=False,
    )
```

```python
import jax
import jax.numpy as jnp
from jax import lax
from jax.experimental import pallas as pl
from jax.experimental.pallas import tpu as pltpu
from jax.sharding import Mesh
from jax.sharding import PartitionSpec as P

SIZES = {"zh": 2, "core": 2, "y": 4, "zl": 8, "x": 4}
AXES = tuple(SIZES)
GROUP = ("zh", "zl", "y", "x")
PASSES = 14
HIGHEST = lax.Precision.HIGHEST
IN_VMEM = pl.BlockSpec(memory_space=pltpu.VMEM)
IN_SMEM = pl.BlockSpec(memory_space=pltpu.SMEM)


def index_map(order):
    count = order.shape[0]
    values = jnp.arange(2**count, dtype=jnp.int32)
    places = jnp.arange(count, dtype=jnp.int32)
    bits = values[:, None] >> places[None, :] & 1
    return jnp.sum(bits << order[None, :], axis=1)


def permuted(gate, where):
    pick = (where[:, None] == jnp.arange(gate.shape[-1])[None, :]).astype(gate.dtype)
    half = jnp.einsum("ai,cij->caj", pick, gate, precision=HIGHEST)
    return jnp.einsum("caj,bj->cab", half, pick, precision=HIGHEST)


def product(left, right):
    def prod(a, b):
        return jnp.dot(a, b, precision=HIGHEST)

    return jnp.stack(
        [
            prod(left[0], right[0]) - prod(left[1], right[1]),
            prod(left[0], right[1]) + prod(left[1], right[0]),
        ]
    )


def as_real(matrix):
    return jnp.concatenate(
        [
            jnp.concatenate([matrix[0], -matrix[1]], axis=1),
            jnp.concatenate([matrix[1], matrix[0]], axis=1),
        ],
        axis=0,
    )


def split(value):
    top = value.astype(jnp.bfloat16)
    return top, (value - top.astype(jnp.float32)).astype(jnp.bfloat16)


def dot3(left, right):
    def prod(a, b):
        return jnp.dot(a, b, preferred_element_type=jnp.float32)

    (left_top, left_rest), (right_top, right_rest) = split(left), split(right)
    return prod(left_top, right_rest) + prod(left_rest, right_top) + prod(left_top, right_top)


def combine(mine, other, own, cross):
    return (
        own[0] * mine[0] - own[1] * mine[1] + (cross[0] * other[0] - cross[1] * other[1]),
        own[0] * mine[1] + own[1] * mine[0] + (cross[0] * other[1] + cross[1] * other[0]),
    )


def first_kernel(passes_ref, unit_ref, mine_ref, other_ref, out_ref):
    half = mine_ref.shape[1]
    own = (unit_ref[0:1, :], unit_ref[1:2, :])
    cross = (unit_ref[2:3, :], unit_ref[3:4, :])

    def one_pass(_, carry):
        parts = combine(
            (mine_ref[0], mine_ref[1]), (other_ref[0], other_ref[1]), own, cross
        )
        for c in range(2):
            out_ref[pl.ds(c, half, 2), :] = parts[c]
        return carry

    lax.fori_loop(0, passes_ref[0], one_pass, 0)


def middle_kernel(moved_ref, unit_ref, mid_ref, low_ref, out_ref):
    rows, order = moved_ref.shape
    size = mid_ref.shape[0] // 2

    def place(level, pair, c):
        return pl.ds(level * size * 4 + pair * 2 + c, size, 4)

    columns = []
    for pair in range(2):
        parts = [
            tuple(moved_ref[place(level, pair, c), :] for c in range(2)) for level in range(2)
        ]
        for level in range(2):
            row = level * 4
            own = (unit_ref[row : row + 1, :], unit_ref[row + 1 : row + 2, :])
            cross = (unit_ref[row + 2 : row + 3, :], unit_ref[row + 3 : row + 4, :])
            columns.append(
                jnp.concatenate(combine(parts[level], parts[1 - level], own, cross), axis=0)
            )
    mixed = dot3(mid_ref[...], jnp.concatenate(columns, axis=1))
    turned = jnp.concatenate(
        [
            jnp.concatenate(
                [
                    mixed[c * size : (c + 1) * size, at * order : (at + 1) * order]
                    for c in range(2)
                ],
                axis=1,
            )
            for at in range(4)
        ],
        axis=0,
    )
    last = dot3(turned, low_ref[...])
    for pair in range(2):
        for level in range(2):
            at = (pair * 2 + level) * size
            for c in range(2):
                out_ref[place(level, pair, c), :] = last[
                    at : at + size, c * order : (c + 1) * order
                ]


def last_kernel(rows_ref, out_ref):
    half = out_ref.shape[1]
    for c in range(2):
        out_ref[c] = rows_ref[pl.ds(c, half, 2), :]


def call(kernel, shape, *operands, specs=None):
    return pl.pallas_call(
        kernel,
        out_shape=jax.ShapeDtypeStruct(shape, jnp.float32),
        in_specs=specs or [IN_VMEM] * len(operands),
        out_specs=IN_VMEM,
        compiler_params=pltpu.CompilerParams(vmem_limit_bytes=32 * 2**20),
    )(*operands)


def exchange(rows):
    moved = lax.all_to_all(rows.reshape(256, 4, -1), GROUP, 0, 0, tiled=True)
    return moved.reshape(rows.shape)


def level_units(unit, order):
    rows = jnp.stack(
        [unit[c, level, level ^ flip] for level in range(2) for flip in range(2) for c in range(2)]
    )
    return jnp.broadcast_to(rows[:, None], (8, order))


def body(state, low_gates, low_order, high_gates, mid_gate, mid_order):
    order = state.shape[3]
    pairs = state.shape[1] * state.shape[2]
    core = lax.axis_index("core")

    mine = state.reshape(2, pairs, order)
    other = lax.ppermute(mine, "core", [(0, 1), (1, 0)])
    both = level_units(high_gates[0], order)
    unit = jnp.where(core == 0, both, jnp.roll(both, 4, axis=0))
    passes = jnp.where(core == 0, 1, PASSES).astype(jnp.int32).reshape(1)
    sent = call(
        first_kernel,
        (2 * pairs, order),
        passes,
        unit,
        mine,
        other,
        specs=[IN_SMEM] + [IN_VMEM] * 3,
    )
    moved = exchange(sent)

    low = product(
        permuted(low_gates[1], index_map(low_order[1])),
        permuted(low_gates[0], index_map(low_order[0])),
    )
    where = index_map(mid_order).reshape(4, 8, 4).transpose(1, 0, 2).reshape(-1)
    mid = permuted(mid_gate, where)
    done = call(
        middle_kernel,
        moved.shape,
        moved,
        level_units(high_gates[1], order),
        as_real(mid),
        as_real(low).T,
    )
    back = exchange(done)
    return call(last_kernel, (2, pairs, order), back).reshape(state.shape)


def solution(mesh):
    mesh = Mesh(mesh.devices.reshape(tuple(SIZES.values())), AXES)
    return jax.shard_map(
        body,
        mesh=mesh,
        in_specs=(P(None, AXES, None, None), P(), P(), P(), P(), P()),
        out_specs=P(None, AXES, None, None),
        check_vma=False,
    )
```

```python
import jax
import jax.numpy as jnp
from jax import lax
from jax.experimental import pallas as pl
from jax.experimental.pallas import tpu as pltpu
from jax.sharding import Mesh
from jax.sharding import PartitionSpec as P

SIZES = {"zh": 2, "core": 2, "y": 4, "zl": 8, "x": 4}
AXES = tuple(SIZES)
GROUP = ("zh", "zl", "y", "x")
PASSES = 90
LATE = 0
HIGHEST = lax.Precision.HIGHEST
IN_VMEM = pl.BlockSpec(memory_space=pltpu.VMEM)
IN_SMEM = pl.BlockSpec(memory_space=pltpu.SMEM)


def split(value):
    top = value.astype(jnp.bfloat16)
    return top, (value - top.astype(jnp.float32)).astype(jnp.bfloat16)


def dot3(left, right):
    def prod(a, b):
        return jnp.dot(a, b, preferred_element_type=jnp.float32)

    (left_top, left_rest), (right_top, right_rest) = split(left), split(right)
    return prod(left_top, right_rest) + prod(left_rest, right_top) + prod(left_top, right_top)


def combine(mine, other, own, cross):
    return (
        own[0] * mine[0] - own[1] * mine[1] + (cross[0] * other[0] - cross[1] * other[1]),
        own[0] * mine[1] + own[1] * mine[0] + (cross[0] * other[1] + cross[1] * other[0]),
    )


def pick_rows(order_ref, at, number):
    count = order_ref.shape[1]
    where = jnp.zeros_like(number)
    for j in range(count):
        where += (number >> j & 1) << order_ref[at, j]
    return (where == lax.broadcasted_iota(jnp.int32, number.shape, 1)).astype(jnp.float32)


def gates_kernel(low_order_ref, mid_order_ref, low_gates_ref, mid_gate_ref, mid_ref, low_ref):
    size = mid_gate_ref.shape[1]
    number = lax.broadcasted_iota(jnp.int32, (size, size), 0)
    group = (number >> 2 & 3) << 5 | (number >> 4 & 7) << 2 | number & 3

    def dot(left, right):
        return jnp.dot(left, right, precision=HIGHEST, preferred_element_type=jnp.float32)

    def permuted(gate, pick):
        half = dot(pick, gate)
        return lax.dot_general(
            half,
            pick,
            (((1,), (1,)), ((), ())),
            precision=HIGHEST,
            preferred_element_type=jnp.float32,
        )

    pick = pick_rows(mid_order_ref, 0, group)
    real, imag = (permuted(mid_gate_ref[c], pick) for c in range(2))
    mid_ref[:size, :size] = real
    mid_ref[:size, size:] = -imag
    mid_ref[size:, :size] = imag
    mid_ref[size:, size:] = real
    lows = []
    for k in range(2):
        pick = pick_rows(low_order_ref, k, number)
        lows.append([permuted(low_gates_ref[k, c], pick) for c in range(2)])
    (right_re, right_im), (left_re, left_im) = lows
    real = (dot(left_re, right_re) - dot(left_im, right_im)).T
    imag = (dot(left_re, right_im) + dot(left_im, right_re)).T
    low_ref[:size, :size] = real
    low_ref[:size, size:] = imag
    low_ref[size:, :size] = -imag
    low_ref[size:, size:] = real


def core_factor(unit_ref, other):
    core = lax.axis_index("core")
    source = 1 - core if other else core
    return tuple(unit_ref[pl.ds(c * 4 + core * 2 + source, 1), :] for c in range(2))


def own_kernel(unit_ref, mine_ref, out_ref):
    re, im = core_factor(unit_ref, False)
    half = mine_ref.shape[1]
    out_ref[pl.ds(0, half, 2), :] = re * mine_ref[0] - im * mine_ref[1]
    out_ref[pl.ds(1, half, 2), :] = re * mine_ref[1] + im * mine_ref[0]


def first_kernel(unit_ref, own_ref, other_ref, out_ref):
    re, im = core_factor(unit_ref, True)
    half = other_ref.shape[1]

    def one_pass(_, carry):
        for c, add in (
            (0, re * other_ref[0] - im * other_ref[1]),
            (1, re * other_ref[1] + im * other_ref[0]),
        ):
            out_ref[pl.ds(c, half, 2), :] = own_ref[pl.ds(c, half, 2), :] + add
        return carry

    late = (lax.axis_index("core") == LATE).astype(jnp.int32)
    lax.fori_loop(0, 1 + late * PASSES, one_pass, 0)


def middle_kernel(moved_ref, unit_ref, mid_ref, low_ref, out_ref):
    rows, order = moved_ref.shape
    size = mid_ref.shape[0] // 2

    def place(level, pair, c):
        return pl.ds(level * size * 4 + pair * 2 + c, size, 4)

    def factor(into, source):
        rows = [8 + c * 4 + into * 2 + source for c in range(2)]
        return tuple(unit_ref[row : row + 1, :] for row in rows)

    columns = []
    for pair in range(2):
        parts = [
            tuple(moved_ref[place(level, pair, c), :] for c in range(2)) for level in range(2)
        ]
        for level in range(2):
            own, cross = factor(level, level), factor(level, 1 - level)
            columns.append(
                jnp.concatenate(combine(parts[level], parts[1 - level], own, cross), axis=0)
            )
    mixed = dot3(mid_ref[...], jnp.concatenate(columns, axis=1))
    turned = jnp.concatenate(
        [
            jnp.concatenate(
                [
                    mixed[c * size : (c + 1) * size, at * order : (at + 1) * order]
                    for c in range(2)
                ],
                axis=1,
            )
            for at in range(4)
        ],
        axis=0,
    )
    last = dot3(turned, low_ref[...])
    for pair in range(2):
        for level in range(2):
            at = (pair * 2 + level) * size
            for c in range(2):
                out_ref[place(level, pair, c), :] = last[
                    at : at + size, c * order : (c + 1) * order
                ]


def last_kernel(rows_ref, out_ref):
    half = out_ref.shape[1]
    for c in range(2):
        out_ref[c] = rows_ref[pl.ds(c, half, 2), :]


def call(kernel, shapes, *operands, specs=None):
    out = jax.tree.map(
        lambda shape: jax.ShapeDtypeStruct(shape, jnp.float32),
        shapes,
        is_leaf=lambda shape: isinstance(shape, tuple),
    )
    return pl.pallas_call(
        kernel,
        out_shape=out,
        in_specs=specs or [IN_VMEM] * len(operands),
        out_specs=jax.tree.map(lambda _: IN_VMEM, out),
        compiler_params=pltpu.CompilerParams(vmem_limit_bytes=32 * 2**20),
    )(*operands)


def exchange(rows):
    moved = lax.all_to_all(rows.reshape(256, 4, -1), GROUP, 0, 0, tiled=True)
    return moved.reshape(rows.shape)


def body(state, low_gates, low_order, high_gates, mid_gate, mid_order):
    order = state.shape[3]
    pairs = state.shape[1] * state.shape[2]
    rows = (2 * pairs, order)

    mine = state.reshape(2, pairs, order)
    other = lax.ppermute(mine, "core", [(0, 1), (1, 0)])
    units = jnp.broadcast_to(high_gates.reshape(16, 1), (16, order))
    own = call(own_kernel, rows, units, mine)
    sent = call(first_kernel, rows, units, own, other)
    sent, low_gates, low_order, mid_gate, mid_order = lax.optimization_barrier(
        (sent, low_gates, low_order, mid_gate, mid_order)
    )
    moved = exchange(sent)
    mid, low = call(
        gates_kernel,
        [(2 * order, 2 * order)] * 2,
        low_order,
        mid_order.reshape(1, -1),
        low_gates,
        mid_gate,
        specs=[IN_SMEM] * 2 + [IN_VMEM] * 2,
    )
    done = call(middle_kernel, rows, moved, units, mid, low)
    back = exchange(done)
    return call(last_kernel, (2, pairs, order), back).reshape(state.shape)


def solution(mesh):
    mesh = Mesh(mesh.devices.reshape(tuple(SIZES.values())), AXES)
    return jax.shard_map(
        body,
        mesh=mesh,
        in_specs=(P(None, AXES, None, None), P(), P(), P(), P(), P()),
        out_specs=P(None, AXES, None, None),
        check_vma=False,
    )
```

```python
import jax
import jax.numpy as jnp
import numpy as np
from jax import lax
from jax.experimental import pallas as pl
from jax.experimental.pallas import tpu as pltpu
from jax.sharding import Mesh
from jax.sharding import PartitionSpec as P

AXIS = "device"
NUMBERS = np.arange(512).reshape(2, 2, 4, 8, 4).transpose(1, 0, 3, 2, 4).reshape(2, 16, 16)
LINES = [[group.tolist() for group in NUMBERS[core].T] for core in range(2)]
PLANES = [[group.tolist() for group in NUMBERS[core]] for core in range(2)]
STAGES = (LINES[0] + PLANES[1], PLANES[0] + LINES[1])
HIGHEST = lax.Precision.HIGHEST
IN_VMEM = pl.BlockSpec(memory_space=pltpu.VMEM)
IN_SMEM = pl.BlockSpec(memory_space=pltpu.SMEM)


def split(value):
    top = value.astype(jnp.bfloat16)
    return top, (value - top.astype(jnp.float32)).astype(jnp.bfloat16)


def dot3(left, right):
    def prod(a, b):
        return jnp.dot(a, b, preferred_element_type=jnp.float32)

    (left_top, left_rest), (right_top, right_rest) = split(left), split(right)
    return prod(left_top, right_rest) + prod(left_rest, right_top) + prod(left_top, right_top)


def core_of():
    return lax.axis_index(AXIS) >> 7 & 1


def pick_rows(order_ref, at, number, columns):
    where = jnp.zeros_like(number)
    for j in range(order_ref.shape[1]):
        where += (number >> j & 1) << order_ref[at, j]
    return (where == lax.broadcasted_iota(jnp.int32, columns, 1)).astype(jnp.float32)


def gates_kernel(
    low_order_ref, mid_order_ref, unit_ref, low_gates_ref, mid_gate_ref, mid_ref, low_ref
):
    size = mid_gate_ref.shape[1]
    group = 2 * size
    lines = core_of() == 0

    def parts(number):
        plane = jnp.where(lines, number >> 4, number & 15)
        line = jnp.where(lines, number & 15, number >> 4)
        return line >> 3, (plane >> 2) << 5 | (line & 7) << 2 | plane & 3

    def dot(left, right):
        return jnp.dot(left, right, precision=HIGHEST, preferred_element_type=jnp.float32)

    def permuted(gate, pick):
        return lax.dot_general(
            dot(pick, gate),
            pick,
            (((1,), (1,)), ((), ())),
            precision=HIGHEST,
            preferred_element_type=jnp.float32,
        )

    into, index = parts(lax.broadcasted_iota(jnp.int32, (group, size), 0))
    pick = pick_rows(mid_order_ref, 0, index, (group, size))
    mid_re, mid_im = (permuted(mid_gate_ref[c], pick) for c in range(2))
    into, _ = parts(lax.broadcasted_iota(jnp.int32, (group, group), 0))
    source, _ = parts(lax.broadcasted_iota(jnp.int32, (group, group), 1))

    def factor(c):
        rows = [
            jnp.concatenate([unit_ref[row : row + 1, :]] * 2, axis=1)
            for row in range(8 + c * 4, 12 + c * 4)
        ]
        return jnp.where(
            into == 0,
            jnp.where(source == 0, rows[0], rows[1]),
            jnp.where(source == 0, rows[2], rows[3]),
        )

    unit_re, unit_im = factor(0), factor(1)
    real = unit_re * mid_re - unit_im * mid_im
    imag = unit_re * mid_im + unit_im * mid_re
    mid_ref[:group, :group] = real
    mid_ref[:group, group:] = -imag
    mid_ref[group:, :group] = imag
    mid_ref[group:, group:] = real

    number = lax.broadcasted_iota(jnp.int32, (size, size), 0)
    lows = []
    for k in range(2):
        pick = pick_rows(low_order_ref, k, number, (size, size))
        lows.append([permuted(low_gates_ref[k, c], pick) for c in range(2)])
    (right_re, right_im), (left_re, left_im) = lows
    real = (dot(left_re, right_re) - dot(left_im, right_im)).T
    imag = (dot(left_re, right_im) + dot(left_im, right_re)).T
    low_ref[:size, :size] = real
    low_ref[:size, size:] = imag
    low_ref[size:, :size] = -imag
    low_ref[size:, size:] = real


def core_factor(unit_ref, other):
    core = core_of()
    source = 1 - core if other else core
    return tuple(unit_ref[pl.ds(c * 4 + core * 2 + source, 1), :] for c in range(2))


def own_kernel(unit_ref, mine_ref, out_ref):
    re, im = core_factor(unit_ref, False)
    half = mine_ref.shape[1]
    out_ref[pl.ds(0, half, 2), :] = re * mine_ref[0] - im * mine_ref[1]
    out_ref[pl.ds(1, half, 2), :] = re * mine_ref[1] + im * mine_ref[0]


def first_kernel(unit_ref, own_ref, other_ref, out_ref):
    re, im = core_factor(unit_ref, True)
    half = other_ref.shape[1]
    for c, add in (
        (0, re * other_ref[0] - im * other_ref[1]),
        (1, re * other_ref[1] + im * other_ref[0]),
    ):
        out_ref[pl.ds(c, half, 2), :] = own_ref[pl.ds(c, half, 2), :] + add


def middle_kernel(moved_ref, mid_ref, low_ref, out_ref):
    rows, order = moved_ref.shape
    size = rows // 4

    def place(pair, c):
        return pl.ds(pair * 2 + c, size, 4)

    stacked = jnp.concatenate(
        [
            jnp.concatenate([moved_ref[place(pair, c), :] for pair in range(2)], axis=1)
            for c in range(2)
        ],
        axis=0,
    )
    mixed = dot3(mid_ref[...], stacked)
    turned = jnp.concatenate(
        [
            jnp.concatenate(
                [
                    mixed[c * size : (c + 1) * size, pair * order : (pair + 1) * order]
                    for c in range(2)
                ],
                axis=1,
            )
            for pair in range(2)
        ],
        axis=0,
    )
    last = dot3(turned, low_ref[...])
    for pair in range(2):
        for c in range(2):
            out_ref[place(pair, c), :] = last[
                pair * size : (pair + 1) * size, c * order : (c + 1) * order
            ]


def last_kernel(rows_ref, out_ref):
    half = out_ref.shape[1]
    for c in range(2):
        out_ref[c] = rows_ref[pl.ds(c, half, 2), :]


def call(kernel, shapes, *operands, specs=None):
    out = jax.tree.map(
        lambda shape: jax.ShapeDtypeStruct(shape, jnp.float32),
        shapes,
        is_leaf=lambda shape: isinstance(shape, tuple),
    )
    return pl.pallas_call(
        kernel,
        out_shape=out,
        in_specs=specs or [IN_VMEM] * len(operands),
        out_specs=jax.tree.map(lambda _: IN_VMEM, out),
        compiler_params=pltpu.CompilerParams(vmem_limit_bytes=32 * 2**20),
    )(*operands)


def exchange(rows, stages):
    blocks = rows.reshape(16, 64, -1)
    blocks = lax.all_to_all(blocks, AXIS, 0, 0, axis_index_groups=stages[0], tiled=True)
    blocks = blocks.reshape(16, 16, 4, -1).transpose(1, 0, 2, 3).reshape(16, 64, -1)
    blocks = lax.all_to_all(blocks, AXIS, 0, 0, axis_index_groups=stages[1], tiled=True)
    return blocks.reshape(rows.shape)


def body(state, low_gates, low_order, high_gates, mid_gate, mid_order):
    order = state.shape[3]
    pairs = state.shape[1] * state.shape[2]
    rows = (2 * pairs, order)

    mine = state.reshape(2, pairs, order)
    other = lax.ppermute(mine, AXIS, [(number, number ^ 128) for number in range(512)])
    units = jnp.broadcast_to(high_gates.reshape(16, 1), (16, order))
    own = call(own_kernel, rows, units, mine)
    sent = call(first_kernel, rows, units, own, other)
    sent, low_gates, low_order, mid_gate, mid_order = lax.optimization_barrier(
        (sent, low_gates, low_order, mid_gate, mid_order)
    )
    moved = exchange(sent, STAGES)
    mid, low = call(
        gates_kernel,
        [(4 * order, 4 * order), (2 * order, 2 * order)],
        low_order,
        mid_order.reshape(1, -1),
        units,
        low_gates,
        mid_gate,
        specs=[IN_SMEM] * 2 + [IN_VMEM] * 3,
    )
    done = call(middle_kernel, rows, moved, mid, low)
    back = exchange(done, STAGES[::-1])
    return call(last_kernel, (2, pairs, order), back).reshape(state.shape)


def solution(mesh):
    return jax.shard_map(
        body,
        mesh=Mesh(mesh.devices.reshape(-1), (AXIS,)),
        in_specs=(P(None, AXIS, None, None), P(), P(), P(), P(), P()),
        out_specs=P(None, AXIS, None, None),
        check_vma=False,
    )
```

```python
import jax
import jax.numpy as jnp
import numpy as np
from jax import lax
from jax.experimental import pallas as pl
from jax.experimental.pallas import tpu as pltpu
from jax.sharding import Mesh
from jax.sharding import PartitionSpec as P

AXIS = "device"
NUMBERS = np.arange(512).reshape(2, 2, 4, 8, 4).transpose(1, 0, 3, 2, 4).reshape(2, 16, 16)
LINES = [[group.tolist() for group in NUMBERS[core].T] for core in range(2)]
PLACES = [k ^ k >> 2 for k in range(16)]
PLANES = [[group[PLACES].tolist() for group in NUMBERS[core]] for core in range(2)]
STAGES = (LINES[0] + PLANES[1], PLANES[0] + LINES[1])
HIGHEST = lax.Precision.HIGHEST
IN_VMEM = pl.BlockSpec(memory_space=pltpu.VMEM)
IN_SMEM = pl.BlockSpec(memory_space=pltpu.SMEM)


def split(value):
    top = value.astype(jnp.bfloat16)
    return top, (value - top.astype(jnp.float32)).astype(jnp.bfloat16)


def bf16_dot(left, right):
    return jnp.dot(left, right, preferred_element_type=jnp.float32)


def dot3(left, right):
    return (
        bf16_dot(left[0], right[1]) + bf16_dot(left[1], right[0]) + bf16_dot(left[0], right[0])
    )


def pick_dot(left, right):
    on_left = left.dtype == jnp.bfloat16
    value = right if on_left else left
    total = None
    for _ in range(3):
        part = value.astype(jnp.bfloat16)
        value = value - part.astype(jnp.float32)
        term = (
            bf16_dot(left, part)
            if on_left
            else lax.dot_general(
                part, right, (((1,), (1,)), ((), ())), preferred_element_type=jnp.float32
            )
        )
        total = term if total is None else total + term
    return total


def store_split(ref, *quarters):
    size = quarters[0].shape[0]
    for at, quarter in enumerate(quarters):
        rows, columns = (pl.ds(place * size, size) for place in (at // 2, at % 2))
        for part, value in enumerate(split(quarter)):
            ref[part, rows, columns] = value


def core_of():
    return lax.axis_index(AXIS) >> 7 & 1


def pick_rows(order_ref, at, number, columns):
    where = jnp.zeros_like(number)
    for j in range(order_ref.shape[1]):
        where += (number >> j & 1) << order_ref[at, j]
    return (where == lax.broadcasted_iota(jnp.int32, columns, 1)).astype(jnp.float32)


def gates_kernel(
    low_order_ref, mid_order_ref, unit_ref, low_gates_ref, mid_gate_ref, mid_ref, low_ref
):
    size = mid_gate_ref.shape[1]
    group = 2 * size
    lines = core_of() == 0

    def parts(number):
        plane = jnp.where(lines, number >> 4, number & 15)
        plane = plane ^ plane >> 2
        line = jnp.where(lines, number & 15, number >> 4)
        return line >> 3, (plane >> 2) << 5 | (line & 7) << 2 | plane & 3

    def permuted(gate, pick):
        chosen = pick.astype(jnp.bfloat16)
        half = pick_dot(chosen, jnp.concatenate([gate[0], gate[1]], axis=1))
        count = gate.shape[2]
        stacked = jnp.concatenate([half[:, :count], half[:, count:]], axis=0)
        whole = pick_dot(stacked, chosen)
        return whole[: pick.shape[0]], whole[pick.shape[0] :]

    into, index = parts(lax.broadcasted_iota(jnp.int32, (group, size), 0))
    pick = pick_rows(mid_order_ref, 0, index, (group, size))
    mid_re, mid_im = permuted(mid_gate_ref, pick)
    into, _ = parts(lax.broadcasted_iota(jnp.int32, (group, group), 0))
    source, _ = parts(lax.broadcasted_iota(jnp.int32, (group, group), 1))

    def factor(c):
        rows = [
            jnp.concatenate([unit_ref[row : row + 1, :]] * 2, axis=1)
            for row in range(8 + c * 4, 12 + c * 4)
        ]
        return jnp.where(
            into == 0,
            jnp.where(source == 0, rows[0], rows[1]),
            jnp.where(source == 0, rows[2], rows[3]),
        )

    unit_re, unit_im = factor(0), factor(1)
    real = unit_re * mid_re - unit_im * mid_im
    imag = unit_re * mid_im + unit_im * mid_re
    store_split(mid_ref, real, -imag, imag, real)

    number = lax.broadcasted_iota(jnp.int32, (size, size), 0)
    right, left = (
        permuted(low_gates_ref[k], pick_rows(low_order_ref, k, number, (size, size)))
        for k in range(2)
    )
    left = jnp.concatenate(
        [
            jnp.concatenate([left[0], -left[1]], axis=1),
            jnp.concatenate([left[1], left[0]], axis=1),
        ],
        axis=0,
    )
    both = jnp.dot(
        left,
        jnp.concatenate(right, axis=0),
        precision=HIGHEST,
        preferred_element_type=jnp.float32,
    )
    real, imag = both[:size].T, both[size:].T
    store_split(low_ref, real, imag, -imag, real)


def core_factor(unit_ref, other):
    core = core_of()
    source = 1 - core if other else core
    return tuple(unit_ref[pl.ds(c * 4 + core * 2 + source, 1), :] for c in range(2))


def own_kernel(unit_ref, mine_ref, out_ref):
    re, im = core_factor(unit_ref, False)
    half = mine_ref.shape[1]
    out_ref[pl.ds(0, half, 2), :] = re * mine_ref[0] - im * mine_ref[1]
    out_ref[pl.ds(1, half, 2), :] = re * mine_ref[1] + im * mine_ref[0]


def first_kernel(unit_ref, own_ref, other_ref, out_ref):
    re, im = core_factor(unit_ref, True)
    half = other_ref.shape[1]
    for c, add in (
        (0, re * other_ref[0] - im * other_ref[1]),
        (1, re * other_ref[1] + im * other_ref[0]),
    ):
        out_ref[pl.ds(c, half, 2), :] = own_ref[pl.ds(c, half, 2), :] + add


def middle_kernel(moved_ref, mid_ref, low_ref, out_ref):
    rows, order = moved_ref.shape
    size = rows // 4

    def place(pair, c):
        return pl.ds(pair * 2 + c, size, 4)

    stacked = jnp.concatenate(
        [
            jnp.concatenate([moved_ref[place(pair, c), :] for pair in range(2)], axis=1)
            for c in range(2)
        ],
        axis=0,
    )
    mixed = dot3((mid_ref[0], mid_ref[1]), split(stacked))
    turned = jnp.concatenate(
        [
            jnp.concatenate(
                [
                    mixed[c * size : (c + 1) * size, pair * order : (pair + 1) * order]
                    for c in range(2)
                ],
                axis=1,
            )
            for pair in range(2)
        ],
        axis=0,
    )
    last = dot3(split(turned), (low_ref[0], low_ref[1]))
    for pair in range(2):
        for c in range(2):
            out_ref[place(pair, c), :] = last[
                pair * size : (pair + 1) * size, c * order : (c + 1) * order
            ]


def last_kernel(rows_ref, out_ref):
    half = out_ref.shape[1]
    for c in range(2):
        out_ref[c] = rows_ref[pl.ds(c, half, 2), :]


def call(kernel, out, *operands, specs=None):
    return pl.pallas_call(
        kernel,
        out_shape=out,
        in_specs=specs or [IN_VMEM] * len(operands),
        out_specs=jax.tree.map(lambda _: IN_VMEM, out),
        compiler_params=pltpu.CompilerParams(vmem_limit_bytes=32 * 2**20),
    )(*operands)


def exchange(rows, stages):
    blocks = rows.reshape(16, 64, -1)
    blocks = lax.all_to_all(blocks, AXIS, 0, 0, axis_index_groups=stages[0], tiled=True)
    blocks = blocks.reshape(16, 16, 4, -1).transpose(1, 0, 2, 3).reshape(16, 64, -1)
    blocks = lax.all_to_all(blocks, AXIS, 0, 0, axis_index_groups=stages[1], tiled=True)
    return blocks.reshape(rows.shape)


def body(state, low_gates, low_order, high_gates, mid_gate, mid_order):
    order = state.shape[3]
    pairs = state.shape[1] * state.shape[2]
    rows = jax.ShapeDtypeStruct((2 * pairs, order), jnp.float32)

    mine = state.reshape(2, pairs, order)
    other = lax.ppermute(mine, AXIS, [(number, number ^ 128) for number in range(512)])
    units = jnp.broadcast_to(high_gates.reshape(16, 1), (16, order))
    own = call(own_kernel, rows, units, mine)
    sent = call(first_kernel, rows, units, own, other)
    moved = exchange(sent, STAGES)
    mid, low = call(
        gates_kernel,
        [
            jax.ShapeDtypeStruct((2, size * order, size * order), jnp.bfloat16)
            for size in (4, 2)
        ],
        low_order,
        mid_order.reshape(1, -1),
        units,
        low_gates,
        mid_gate,
        specs=[IN_SMEM] * 2 + [IN_VMEM] * 3,
    )
    done = call(middle_kernel, rows, moved, mid, low)
    back = exchange(done, STAGES[::-1])
    final = jax.ShapeDtypeStruct(mine.shape, jnp.float32)
    return call(last_kernel, final, back).reshape(state.shape)


def solution(mesh):
    return jax.shard_map(
        body,
        mesh=Mesh(mesh.devices.reshape(-1), (AXIS,)),
        in_specs=(P(None, AXIS, None, None), P(), P(), P(), P(), P()),
        out_specs=P(None, AXIS, None, None),
        check_vma=False,
    )
```

```python
import jax
import jax.numpy as jnp
import numpy as np
from jax import lax
from jax.experimental import pallas as pl
from jax.experimental.pallas import tpu as pltpu
from jax.sharding import Mesh
from jax.sharding import PartitionSpec as P

AXIS = "device"
NUMBERS = np.arange(512).reshape(2, 2, 4, 8, 4).transpose(1, 0, 3, 2, 4).reshape(2, 16, 16)
LINES = [[group.tolist() for group in NUMBERS[core].T] for core in range(2)]
PLACES = [k ^ k >> 2 for k in range(16)]
PLANES = [[group[PLACES].tolist() for group in NUMBERS[core]] for core in range(2)]
STAGES = (LINES[0] + PLANES[1], PLANES[0] + LINES[1])
REPEATS = 13
IN_VMEM = pl.BlockSpec(memory_space=pltpu.VMEM)


def split(value):
    top = value.astype(jnp.bfloat16)
    return top, (value - top.astype(jnp.float32)).astype(jnp.bfloat16)


def bf16_dot(left, right):
    return jnp.dot(left, right, preferred_element_type=jnp.float32)


def dot3(left, right):
    return (
        bf16_dot(left[0], right[1]) + bf16_dot(left[1], right[0]) + bf16_dot(left[0], right[0])
    )


def pick_dot(left, right):
    on_left = left.dtype == jnp.bfloat16
    value = right if on_left else left
    total = None
    for _ in range(3):
        part = value.astype(jnp.bfloat16)
        value = value - part.astype(jnp.float32)
        term = (
            bf16_dot(left, part)
            if on_left
            else lax.dot_general(
                part, right, (((1,), (1,)), ((), ())), preferred_element_type=jnp.float32
            )
        )
        total = term if total is None else total + term
    return total


def store_split(ref, *quarters):
    size = quarters[0].shape[0]
    for at, quarter in enumerate(quarters):
        rows, columns = (pl.ds(place * size, size) for place in (at // 2, at % 2))
        for part, value in enumerate(split(quarter)):
            ref[part, rows, columns] = value


def core_of():
    return lax.axis_index(AXIS) >> 7 & 1


def pick_rows(order_ref, at, number, columns):
    where = jnp.zeros_like(number)
    for j in range(order_ref.shape[1]):
        where += (number >> j & 1) << order_ref[at : at + 1, j : j + 1]
    return (where == lax.broadcasted_iota(jnp.int32, columns, 1)).astype(jnp.float32)


def gates_kernel(
    low_order_ref, mid_order_ref, unit_ref, low_gates_ref, mid_gate_ref, mid_ref, low_ref
):
    size = mid_gate_ref.shape[1]
    group = 2 * size
    lines = core_of() == 0

    def parts(number):
        plane = jnp.where(lines, number >> 4, number & 15)
        plane = plane ^ plane >> 2
        line = jnp.where(lines, number & 15, number >> 4)
        return line >> 3, (plane >> 2) << 5 | (line & 7) << 2 | plane & 3

    def permuted(gate, pick):
        chosen = pick.astype(jnp.bfloat16)
        half = pick_dot(chosen, jnp.concatenate([gate[0], gate[1]], axis=1))
        count = gate.shape[2]
        stacked = jnp.concatenate([half[:, :count], half[:, count:]], axis=0)
        whole = pick_dot(stacked, chosen)
        return whole[: pick.shape[0]], whole[pick.shape[0] :]

    into, index = parts(lax.broadcasted_iota(jnp.int32, (group, size), 0))
    pick = pick_rows(mid_order_ref, 0, index, (group, size))
    mid_re, mid_im = permuted(mid_gate_ref, pick)
    into, _ = parts(lax.broadcasted_iota(jnp.int32, (group, group), 0))
    source, _ = parts(lax.broadcasted_iota(jnp.int32, (group, group), 1))

    def factor(c):
        rows = [
            jnp.concatenate([unit_ref[row : row + 1, :]] * 2, axis=1)
            for row in range(8 + c * 4, 12 + c * 4)
        ]
        return jnp.where(
            into == 0,
            jnp.where(source == 0, rows[0], rows[1]),
            jnp.where(source == 0, rows[2], rows[3]),
        )

    unit_re, unit_im = factor(0), factor(1)
    real = unit_re * mid_re - unit_im * mid_im
    imag = unit_re * mid_im + unit_im * mid_re
    store_split(mid_ref, real, -imag, imag, real)

    number = lax.broadcasted_iota(jnp.int32, (size, size), 0)
    right, left = (
        permuted(low_gates_ref[k], pick_rows(low_order_ref, k, number, (size, size)))
        for k in range(2)
    )
    left = jnp.concatenate(
        [
            jnp.concatenate([left[0], -left[1]], axis=1),
            jnp.concatenate([left[1], left[0]], axis=1),
        ],
        axis=0,
    )
    both = dot3(split(left), split(jnp.concatenate(right, axis=0)))
    real, imag = both[:size].T, both[size:].T
    store_split(low_ref, real, imag, -imag, real)


def core_factor(unit_ref, other):
    core = core_of()
    source = 1 - core if other else core
    return tuple(unit_ref[pl.ds(c * 4 + core * 2 + source, 1), :] for c in range(2))


def own_kernel(unit_ref, mine_ref, out_ref):
    re, im = core_factor(unit_ref, False)
    half = mine_ref.shape[1]
    out_ref[pl.ds(0, half, 2), :] = re * mine_ref[0] - im * mine_ref[1]
    out_ref[pl.ds(1, half, 2), :] = re * mine_ref[1] + im * mine_ref[0]


def first_kernel(unit_ref, own_ref, other_ref, out_ref):
    re, im = core_factor(unit_ref, True)
    half = other_ref.shape[1]

    def store(_, carry):
        for c, add in (
            (0, re * other_ref[0] - im * other_ref[1]),
            (1, re * other_ref[1] + im * other_ref[0]),
        ):
            out_ref[pl.ds(c, half, 2), :] = own_ref[pl.ds(c, half, 2), :] + add
        return carry

    lax.fori_loop(0, 1 + REPEATS * core_of(), store, 0)


def middle_kernel(moved_ref, mid_ref, low_ref, out_ref):
    rows, order = moved_ref.shape
    size = rows // 4

    def place(pair, c):
        return pl.ds(pair * 2 + c, size, 4)

    stacked = jnp.concatenate(
        [
            jnp.concatenate([moved_ref[place(pair, c), :] for pair in range(2)], axis=1)
            for c in range(2)
        ],
        axis=0,
    )
    mixed = dot3((mid_ref[0], mid_ref[1]), split(stacked))
    turned = jnp.concatenate(
        [
            jnp.concatenate(
                [
                    mixed[c * size : (c + 1) * size, pair * order : (pair + 1) * order]
                    for c in range(2)
                ],
                axis=1,
            )
            for pair in range(2)
        ],
        axis=0,
    )
    last = dot3(split(turned), (low_ref[0], low_ref[1]))
    for pair in range(2):
        for c in range(2):
            out_ref[place(pair, c), :] = last[
                pair * size : (pair + 1) * size, c * order : (c + 1) * order
            ]


def last_kernel(rows_ref, out_ref):
    half = out_ref.shape[1]
    for c in range(2):
        out_ref[c] = rows_ref[pl.ds(c, half, 2), :]


def call(kernel, out, *operands):
    return pl.pallas_call(
        kernel,
        out_shape=out,
        in_specs=[IN_VMEM] * len(operands),
        out_specs=jax.tree.map(lambda _: IN_VMEM, out),
        compiler_params=pltpu.CompilerParams(vmem_limit_bytes=32 * 2**20),
    )(*operands)


def exchange(rows, stages):
    blocks = rows.reshape(16, 64, -1)
    blocks = lax.all_to_all(blocks, AXIS, 0, 0, axis_index_groups=stages[0], tiled=True)
    blocks = blocks.reshape(16, 16, 4, -1).transpose(1, 0, 2, 3).reshape(16, 64, -1)
    blocks = lax.all_to_all(blocks, AXIS, 0, 0, axis_index_groups=stages[1], tiled=True)
    return blocks.reshape(rows.shape)


def body(state, low_gates, low_order, high_gates, mid_gate, mid_order):
    order = state.shape[3]
    pairs = state.shape[1] * state.shape[2]
    rows = jax.ShapeDtypeStruct((2 * pairs, order), jnp.float32)

    mine = state.reshape(2, pairs, order)
    other = lax.ppermute(mine, AXIS, [(number, number ^ 128) for number in range(512)])
    units = jnp.broadcast_to(high_gates.reshape(16, 1), (16, order))
    own = call(own_kernel, rows, units, mine)
    mid, low = call(
        gates_kernel,
        [
            jax.ShapeDtypeStruct((2, size * order, size * order), jnp.bfloat16)
            for size in (4, 2)
        ],
        low_order,
        mid_order.reshape(1, -1),
        units,
        low_gates,
        mid_gate,
    )
    sent = call(first_kernel, rows, units, own, other)
    moved = exchange(sent, STAGES)
    done = call(middle_kernel, rows, moved, mid, low)
    back = exchange(done, STAGES[::-1])
    final = jax.ShapeDtypeStruct(mine.shape, jnp.float32)
    return call(last_kernel, final, back).reshape(state.shape)


def solution(mesh):
    return jax.shard_map(
        body,
        mesh=Mesh(mesh.devices.reshape(-1), (AXIS,)),
        in_specs=(P(None, AXIS, None, None), P(), P(), P(), P(), P()),
        out_specs=P(None, AXIS, None, None),
        check_vma=False,
    )
```

```python
import jax
import jax.numpy as jnp
import numpy as np
from jax import lax
from jax.experimental import pallas as pl
from jax.experimental.pallas import tpu as pltpu
from jax.sharding import Mesh
from jax.sharding import PartitionSpec as P

AXIS = "device"
NUMBERS = np.arange(512).reshape(2, 2, 4, 8, 4).transpose(1, 0, 3, 2, 4).reshape(2, 16, 16)
LINES = [[group.tolist() for group in NUMBERS[core].T] for core in range(2)]
PLACES = [k ^ (k >> 2 & 1) * 3 for k in range(16)]
PLANES = [[group[PLACES].tolist() for group in NUMBERS[core]] for core in range(2)]
STAGES = (LINES[0] + PLANES[1], PLANES[0] + LINES[1])
IN_VMEM = pl.BlockSpec(memory_space=pltpu.VMEM)


def split(value):
    top = value.astype(jnp.bfloat16)
    return top, (value - top.astype(jnp.float32)).astype(jnp.bfloat16)


def bf16_dot(left, right):
    return jnp.dot(left, right, preferred_element_type=jnp.float32)


def dot3(left, right):
    return (
        bf16_dot(left[0], right[1]) + bf16_dot(left[1], right[0]) + bf16_dot(left[0], right[0])
    )


def pick_dot(left, right):
    on_left = left.dtype == jnp.bfloat16
    value = right if on_left else left
    total = None
    for _ in range(3):
        part = value.astype(jnp.bfloat16)
        value = value - part.astype(jnp.float32)
        term = (
            bf16_dot(left, part)
            if on_left
            else lax.dot_general(
                part, right, (((1,), (1,)), ((), ())), preferred_element_type=jnp.float32
            )
        )
        total = term if total is None else total + term
    return total


def store_split(ref, *quarters):
    size = quarters[0].shape[0]
    for at, quarter in enumerate(quarters):
        rows, columns = (pl.ds(place * size, size) for place in (at // 2, at % 2))
        for part, value in enumerate(split(quarter)):
            ref[part, rows, columns] = value


def core_of():
    return lax.axis_index(AXIS) >> 7 & 1


def pick_rows(order_ref, at, number, columns):
    where = jnp.zeros_like(number)
    for j in range(order_ref.shape[1]):
        where += (number >> j & 1) << order_ref[at : at + 1, j : j + 1]
    return (where == lax.broadcasted_iota(jnp.int32, columns, 1)).astype(jnp.float32)


def gates_kernel(
    low_order_ref, mid_order_ref, unit_ref, low_gates_ref, mid_gate_ref, mid_ref, low_ref
):
    size = mid_gate_ref.shape[1]
    group = 2 * size
    lines = core_of() == 0

    def parts(number):
        plane = jnp.where(lines, number >> 4, number & 15)
        plane = plane ^ (plane >> 2 & 1) * 3
        line = jnp.where(lines, number & 15, number >> 4)
        return line >> 3, (plane >> 2) << 5 | (line & 7) << 2 | plane & 3

    def permuted(gate, pick):
        chosen = pick.astype(jnp.bfloat16)
        half = pick_dot(chosen, jnp.concatenate([gate[0], gate[1]], axis=1))
        count = gate.shape[2]
        stacked = jnp.concatenate([half[:, :count], half[:, count:]], axis=0)
        whole = pick_dot(stacked, chosen)
        return whole[: pick.shape[0]], whole[pick.shape[0] :]

    into, index = parts(lax.broadcasted_iota(jnp.int32, (group, size), 0))
    pick = pick_rows(mid_order_ref, 0, index, (group, size))
    mid_re, mid_im = permuted(mid_gate_ref, pick)
    into, _ = parts(lax.broadcasted_iota(jnp.int32, (group, group), 0))
    source, _ = parts(lax.broadcasted_iota(jnp.int32, (group, group), 1))

    def factor(c):
        rows = [
            jnp.concatenate([unit_ref[row : row + 1, :]] * 2, axis=1)
            for row in range(8 + c * 4, 12 + c * 4)
        ]
        return jnp.where(
            into == 0,
            jnp.where(source == 0, rows[0], rows[1]),
            jnp.where(source == 0, rows[2], rows[3]),
        )

    unit_re, unit_im = factor(0), factor(1)
    real = unit_re * mid_re - unit_im * mid_im
    imag = unit_re * mid_im + unit_im * mid_re
    store_split(mid_ref, real, -imag, imag, real)

    number = lax.broadcasted_iota(jnp.int32, (size, size), 0)
    right, left = (
        permuted(low_gates_ref[k], pick_rows(low_order_ref, k, number, (size, size)))
        for k in range(2)
    )
    left = jnp.concatenate(
        [
            jnp.concatenate([left[0], -left[1]], axis=1),
            jnp.concatenate([left[1], left[0]], axis=1),
        ],
        axis=0,
    )
    both = dot3(split(left), split(jnp.concatenate(right, axis=0)))
    real, imag = both[:size].T, both[size:].T
    store_split(low_ref, real, imag, -imag, real)


def core_factor(unit_ref, other):
    core = core_of()
    source = 1 - core if other else core
    return tuple(unit_ref[pl.ds(c * 4 + core * 2 + source, 1), :] for c in range(2))


def own_kernel(unit_ref, mine_ref, out_ref):
    re, im = core_factor(unit_ref, False)
    half = mine_ref.shape[1]
    out_ref[pl.ds(0, half, 2), :] = re * mine_ref[0] - im * mine_ref[1]
    out_ref[pl.ds(1, half, 2), :] = re * mine_ref[1] + im * mine_ref[0]


def first_kernel(unit_ref, own_ref, other_ref, out_ref):
    re, im = core_factor(unit_ref, True)
    half = other_ref.shape[1]
    for c, add in (
        (0, re * other_ref[0] - im * other_ref[1]),
        (1, re * other_ref[1] + im * other_ref[0]),
    ):
        out_ref[pl.ds(c, half, 2), :] = own_ref[pl.ds(c, half, 2), :] + add


def middle_kernel(moved_ref, mid_ref, low_ref, out_ref):
    rows, order = moved_ref.shape
    size = rows // 4

    def place(pair, c):
        return pl.ds(pair * 2 + c, size, 4)

    stacked = jnp.concatenate(
        [
            jnp.concatenate([moved_ref[place(pair, c), :] for pair in range(2)], axis=1)
            for c in range(2)
        ],
        axis=0,
    )
    mixed = dot3((mid_ref[0], mid_ref[1]), split(stacked))
    turned = jnp.concatenate(
        [
            jnp.concatenate(
                [
                    mixed[c * size : (c + 1) * size, pair * order : (pair + 1) * order]
                    for c in range(2)
                ],
                axis=1,
            )
            for pair in range(2)
        ],
        axis=0,
    )
    last = dot3(split(turned), (low_ref[0], low_ref[1]))
    for pair in range(2):
        for c in range(2):
            out_ref[place(pair, c), :] = last[
                pair * size : (pair + 1) * size, c * order : (c + 1) * order
            ]


def last_kernel(rows_ref, out_ref):
    half = out_ref.shape[1]
    for c in range(2):
        out_ref[c] = rows_ref[pl.ds(c, half, 2), :]


def call(kernel, out, *operands):
    return pl.pallas_call(
        kernel,
        out_shape=out,
        in_specs=[IN_VMEM] * len(operands),
        out_specs=jax.tree.map(lambda _: IN_VMEM, out),
        compiler_params=pltpu.CompilerParams(vmem_limit_bytes=32 * 2**20),
    )(*operands)


def exchange(rows, stages):
    blocks = rows.reshape(16, 64, -1)
    blocks = lax.all_to_all(blocks, AXIS, 0, 0, axis_index_groups=stages[0], tiled=True)
    blocks = blocks.reshape(16, 16, 4, -1).transpose(1, 0, 2, 3).reshape(16, 64, -1)
    blocks = lax.all_to_all(blocks, AXIS, 0, 0, axis_index_groups=stages[1], tiled=True)
    return blocks.reshape(rows.shape)


def body(state, low_gates, low_order, high_gates, mid_gate, mid_order):
    order = state.shape[3]
    pairs = state.shape[1] * state.shape[2]
    rows = jax.ShapeDtypeStruct((2 * pairs, order), jnp.float32)

    mine = state.reshape(2, pairs, order)
    other = lax.ppermute(mine, AXIS, [(number, number ^ 128) for number in range(512)])
    units = jnp.broadcast_to(high_gates.reshape(16, 1), (16, order))
    own = call(own_kernel, rows, units, mine)
    mid, low = call(
        gates_kernel,
        [
            jax.ShapeDtypeStruct((2, size * order, size * order), jnp.bfloat16)
            for size in (4, 2)
        ],
        low_order,
        mid_order.reshape(1, -1),
        units,
        low_gates,
        mid_gate,
    )
    sent = call(first_kernel, rows, units, own, other)
    moved = exchange(sent, STAGES)
    done = call(middle_kernel, rows, moved, mid, low)
    back = exchange(done, STAGES[::-1])
    final = jax.ShapeDtypeStruct(mine.shape, jnp.float32)
    return call(last_kernel, final, back).reshape(state.shape)


def solution(mesh):
    return jax.shard_map(
        body,
        mesh=Mesh(mesh.devices.reshape(-1), (AXIS,)),
        in_specs=(P(None, AXIS, None, None), P(), P(), P(), P(), P()),
        out_specs=P(None, AXIS, None, None),
        check_vma=False,
    )
```

```python
import jax
import jax.numpy as jnp
import numpy as np
from jax import lax
from jax.experimental import pallas as pl
from jax.experimental.pallas import tpu as pltpu
from jax.sharding import Mesh
from jax.sharding import PartitionSpec as P

AXIS = "device"
NUMBERS = np.arange(512).reshape(2, 2, 4, 8, 4).transpose(1, 0, 3, 2, 4).reshape(2, 16, 16)
LINES = [[group.tolist() for group in NUMBERS[core].T] for core in range(2)]
PLACES = [k ^ (k >> 2 & 1) * 3 for k in range(16)]
PLANES = [[group[PLACES].tolist() for group in NUMBERS[core]] for core in range(2)]
STAGES = (LINES[0] + PLANES[1], PLANES[0] + LINES[1])
REPEATS = 26
IN_VMEM = pl.BlockSpec(memory_space=pltpu.VMEM)


def split(value):
    top = value.astype(jnp.bfloat16)
    return top, (value - top.astype(jnp.float32)).astype(jnp.bfloat16)


def bf16_dot(left, right):
    return jnp.dot(left, right, preferred_element_type=jnp.float32)


def dot3(left, right):
    return (
        bf16_dot(left[0], right[1]) + bf16_dot(left[1], right[0]) + bf16_dot(left[0], right[0])
    )


def pick_dot(left, right):
    on_left = left.dtype == jnp.bfloat16
    value = right if on_left else left
    total = None
    for _ in range(3):
        part = value.astype(jnp.bfloat16)
        value = value - part.astype(jnp.float32)
        term = (
            bf16_dot(left, part)
            if on_left
            else lax.dot_general(
                part, right, (((1,), (1,)), ((), ())), preferred_element_type=jnp.float32
            )
        )
        total = term if total is None else total + term
    return total


def store_split(ref, *quarters):
    size = quarters[0].shape[0]
    for at, quarter in enumerate(quarters):
        rows, columns = (pl.ds(place * size, size) for place in (at // 2, at % 2))
        for part, value in enumerate(split(quarter)):
            ref[part, rows, columns] = value


def core_of():
    return lax.axis_index(AXIS) >> 7 & 1


def pick_rows(order_ref, at, number, columns):
    where = jnp.zeros_like(number)
    for j in range(order_ref.shape[1]):
        where += (number >> j & 1) << order_ref[at : at + 1, j : j + 1]
    return (where == lax.broadcasted_iota(jnp.int32, columns, 1)).astype(jnp.float32)


def gates_kernel(
    low_order_ref, mid_order_ref, unit_ref, low_gates_ref, mid_gate_ref, mid_ref, low_ref
):
    size = mid_gate_ref.shape[1]
    group = 2 * size
    lines = core_of() == 0

    def parts(number):
        plane = jnp.where(lines, number >> 4, number & 15)
        plane = plane ^ (plane >> 2 & 1) * 3
        line = jnp.where(lines, number & 15, number >> 4)
        return line >> 3, (plane >> 2) << 5 | (line & 7) << 2 | plane & 3

    def permuted(gate, pick):
        chosen = pick.astype(jnp.bfloat16)
        half = pick_dot(chosen, jnp.concatenate([gate[0], gate[1]], axis=1))
        count = gate.shape[2]
        stacked = jnp.concatenate([half[:, :count], half[:, count:]], axis=0)
        whole = pick_dot(stacked, chosen)
        return whole[: pick.shape[0]], whole[pick.shape[0] :]

    into, index = parts(lax.broadcasted_iota(jnp.int32, (group, size), 0))
    pick = pick_rows(mid_order_ref, 0, index, (group, size))
    mid_re, mid_im = permuted(mid_gate_ref, pick)
    into, _ = parts(lax.broadcasted_iota(jnp.int32, (group, group), 0))
    source, _ = parts(lax.broadcasted_iota(jnp.int32, (group, group), 1))

    def factor(c):
        rows = [
            jnp.concatenate([unit_ref[row : row + 1, :]] * 2, axis=1)
            for row in range(8 + c * 4, 12 + c * 4)
        ]
        return jnp.where(
            into == 0,
            jnp.where(source == 0, rows[0], rows[1]),
            jnp.where(source == 0, rows[2], rows[3]),
        )

    unit_re, unit_im = factor(0), factor(1)
    real = unit_re * mid_re - unit_im * mid_im
    imag = unit_re * mid_im + unit_im * mid_re
    store_split(mid_ref, real, -imag, imag, real)

    number = lax.broadcasted_iota(jnp.int32, (size, size), 0)
    right, left = (
        permuted(low_gates_ref[k], pick_rows(low_order_ref, k, number, (size, size)))
        for k in range(2)
    )
    left = jnp.concatenate(
        [
            jnp.concatenate([left[0], -left[1]], axis=1),
            jnp.concatenate([left[1], left[0]], axis=1),
        ],
        axis=0,
    )
    both = dot3(split(left), split(jnp.concatenate(right, axis=0)))
    real, imag = both[:size].T, both[size:].T
    store_split(low_ref, real, imag, -imag, real)


def core_factor(unit_ref, other):
    core = core_of()
    source = 1 - core if other else core
    return tuple(unit_ref[pl.ds(c * 4 + core * 2 + source, 1), :] for c in range(2))


def own_kernel(unit_ref, mine_ref, out_ref):
    re, im = core_factor(unit_ref, False)
    half = mine_ref.shape[1]
    out_ref[pl.ds(0, half, 2), :] = re * mine_ref[0] - im * mine_ref[1]
    out_ref[pl.ds(1, half, 2), :] = re * mine_ref[1] + im * mine_ref[0]


def first_kernel(unit_ref, own_ref, other_ref, out_ref):
    re, im = core_factor(unit_ref, True)
    half = other_ref.shape[1]

    def store(_, carry):
        for c, add in (
            (0, re * other_ref[0] - im * other_ref[1]),
            (1, re * other_ref[1] + im * other_ref[0]),
        ):
            out_ref[pl.ds(c, half, 2), :] = own_ref[pl.ds(c, half, 2), :] + add
        return carry

    lax.fori_loop(0, 1 + REPEATS * core_of(), store, 0)


def middle_kernel(moved_ref, mid_ref, low_ref, out_ref):
    rows, order = moved_ref.shape
    size = rows // 4

    def place(pair, c):
        return pl.ds(pair * 2 + c, size, 4)

    stacked = jnp.concatenate(
        [
            jnp.concatenate([moved_ref[place(pair, c), :] for pair in range(2)], axis=1)
            for c in range(2)
        ],
        axis=0,
    )
    mixed = dot3((mid_ref[0], mid_ref[1]), split(stacked))
    turned = jnp.concatenate(
        [
            jnp.concatenate(
                [
                    mixed[c * size : (c + 1) * size, pair * order : (pair + 1) * order]
                    for c in range(2)
                ],
                axis=1,
            )
            for pair in range(2)
        ],
        axis=0,
    )
    last = dot3(split(turned), (low_ref[0], low_ref[1]))
    for pair in range(2):
        for c in range(2):
            out_ref[place(pair, c), :] = last[
                pair * size : (pair + 1) * size, c * order : (c + 1) * order
            ]


def last_kernel(rows_ref, out_ref):
    half = out_ref.shape[1]
    for c in range(2):
        out_ref[c] = rows_ref[pl.ds(c, half, 2), :]


def call(kernel, out, *operands):
    return pl.pallas_call(
        kernel,
        out_shape=out,
        in_specs=[IN_VMEM] * len(operands),
        out_specs=jax.tree.map(lambda _: IN_VMEM, out),
        compiler_params=pltpu.CompilerParams(vmem_limit_bytes=32 * 2**20),
    )(*operands)


def exchange(rows, stages, beside=()):
    blocks = rows.reshape(16, 64, -1)
    blocks = lax.all_to_all(blocks, AXIS, 0, 0, axis_index_groups=stages[0], tiled=True)
    blocks, beside = lax.optimization_barrier((blocks, beside))
    blocks = blocks.reshape(16, 16, 4, -1).transpose(1, 0, 2, 3).reshape(16, 64, -1)
    blocks = lax.all_to_all(blocks, AXIS, 0, 0, axis_index_groups=stages[1], tiled=True)
    return blocks.reshape(rows.shape), beside


def body(state, low_gates, low_order, high_gates, mid_gate, mid_order):
    order = state.shape[3]
    pairs = state.shape[1] * state.shape[2]
    rows = jax.ShapeDtypeStruct((2 * pairs, order), jnp.float32)

    mine = state.reshape(2, pairs, order)
    other = lax.ppermute(mine, AXIS, [(number, number ^ 128) for number in range(512)])
    units = jnp.broadcast_to(high_gates.reshape(16, 1), (16, order))
    own = call(own_kernel, rows, units, mine)
    sent = call(first_kernel, rows, units, own, other)
    sent, low_gates, low_order, mid_gate, mid_order = lax.optimization_barrier(
        (sent, low_gates, low_order, mid_gate, mid_order)
    )
    mid, low = call(
        gates_kernel,
        [
            jax.ShapeDtypeStruct((2, size * order, size * order), jnp.bfloat16)
            for size in (4, 2)
        ],
        low_order,
        mid_order.reshape(1, -1),
        units,
        low_gates,
        mid_gate,
    )
    moved, (mid, low) = exchange(sent, STAGES, (mid, low))
    done = call(middle_kernel, rows, moved, mid, low)
    back, _ = exchange(done, STAGES[::-1])
    final = jax.ShapeDtypeStruct(mine.shape, jnp.float32)
    return call(last_kernel, final, back).reshape(state.shape)


def solution(mesh):
    return jax.shard_map(
        body,
        mesh=Mesh(mesh.devices.reshape(-1), (AXIS,)),
        in_specs=(P(None, AXIS, None, None), P(), P(), P(), P(), P()),
        out_specs=P(None, AXIS, None, None),
        check_vma=False,
    )
```

```python
import jax
import jax.numpy as jnp
import numpy as np
from jax import lax
from jax.experimental import pallas as pl
from jax.experimental.pallas import tpu as pltpu
from jax.sharding import Mesh
from jax.sharding import PartitionSpec as P

AXIS = "device"
NUMBERS = np.arange(512).reshape(2, 2, 4, 8, 4).transpose(1, 0, 3, 2, 4).reshape(2, 16, 16)
LINES = [[group.tolist() for group in NUMBERS[core].T] for core in range(2)]
PLACES = [k ^ (k >> 2 & 1) * 3 for k in range(16)]
PLANES = [[group[PLACES].tolist() for group in NUMBERS[core]] for core in range(2)]
STAGES = (LINES[0] + PLANES[1], PLANES[0] + LINES[1])
REPEATS = 20
IN_VMEM = pl.BlockSpec(memory_space=pltpu.VMEM)


def split(value):
    top = value.astype(jnp.bfloat16)
    return top, (value - top.astype(jnp.float32)).astype(jnp.bfloat16)


def bf16_dot(left, right):
    return jnp.dot(left, right, preferred_element_type=jnp.float32)


def dot3(left, right):
    return (
        bf16_dot(left[0], right[1]) + bf16_dot(left[1], right[0]) + bf16_dot(left[0], right[0])
    )


def pick_dot(left, right):
    on_left = left.dtype == jnp.bfloat16
    value = right if on_left else left
    total = None
    for _ in range(3):
        part = value.astype(jnp.bfloat16)
        value = value - part.astype(jnp.float32)
        term = (
            bf16_dot(left, part)
            if on_left
            else lax.dot_general(
                part, right, (((1,), (1,)), ((), ())), preferred_element_type=jnp.float32
            )
        )
        total = term if total is None else total + term
    return total


def store_split(ref, *quarters):
    size = quarters[0].shape[0]
    for at, quarter in enumerate(quarters):
        rows, columns = (pl.ds(place * size, size) for place in (at // 2, at % 2))
        for part, value in enumerate(split(quarter)):
            ref[part, rows, columns] = value


def core_of():
    return lax.axis_index(AXIS) >> 7 & 1


def pick_rows(order_ref, at, number, columns):
    where = jnp.zeros_like(number)
    for j in range(order_ref.shape[1]):
        where += (number >> j & 1) << order_ref[at : at + 1, j : j + 1]
    return (where == lax.broadcasted_iota(jnp.int32, columns, 1)).astype(jnp.float32)


def gates_kernel(
    low_order_ref, mid_order_ref, unit_ref, low_gates_ref, mid_gate_ref, mid_ref, low_ref
):
    size = mid_gate_ref.shape[1]
    group = 2 * size
    lines = core_of() == 0

    def parts(number):
        plane = jnp.where(lines, number >> 4, number & 15)
        plane = plane ^ (plane >> 2 & 1) * 3
        line = jnp.where(lines, number & 15, number >> 4)
        return line >> 3, (plane >> 2) << 5 | (line & 7) << 2 | plane & 3

    def permuted(gate, pick):
        chosen = pick.astype(jnp.bfloat16)
        half = pick_dot(chosen, jnp.concatenate([gate[0], gate[1]], axis=1))
        count = gate.shape[2]
        stacked = jnp.concatenate([half[:, :count], half[:, count:]], axis=0)
        whole = pick_dot(stacked, chosen)
        return whole[: pick.shape[0]], whole[pick.shape[0] :]

    into, index = parts(lax.broadcasted_iota(jnp.int32, (group, size), 0))
    pick = pick_rows(mid_order_ref, 0, index, (group, size))
    mid_re, mid_im = permuted(mid_gate_ref, pick)
    into, _ = parts(lax.broadcasted_iota(jnp.int32, (group, group), 0))
    source, _ = parts(lax.broadcasted_iota(jnp.int32, (group, group), 1))

    def factor(c):
        rows = [
            jnp.concatenate([unit_ref[row : row + 1, :]] * 2, axis=1)
            for row in range(8 + c * 4, 12 + c * 4)
        ]
        return jnp.where(
            into == 0,
            jnp.where(source == 0, rows[0], rows[1]),
            jnp.where(source == 0, rows[2], rows[3]),
        )

    unit_re, unit_im = factor(0), factor(1)
    real = unit_re * mid_re - unit_im * mid_im
    imag = unit_re * mid_im + unit_im * mid_re
    store_split(mid_ref, real, -imag, imag, real)

    number = lax.broadcasted_iota(jnp.int32, (size, size), 0)
    right, left = (
        permuted(low_gates_ref[k], pick_rows(low_order_ref, k, number, (size, size)))
        for k in range(2)
    )
    left = jnp.concatenate(
        [
            jnp.concatenate([left[0], -left[1]], axis=1),
            jnp.concatenate([left[1], left[0]], axis=1),
        ],
        axis=0,
    )
    both = dot3(split(left), split(jnp.concatenate(right, axis=0)))
    real, imag = both[:size].T, both[size:].T
    store_split(low_ref, real, imag, -imag, real)


def core_factor(unit_ref, other):
    core = core_of()
    source = 1 - core if other else core
    return tuple(unit_ref[pl.ds(c * 4 + core * 2 + source, 1), :] for c in range(2))


def own_kernel(unit_ref, mine_ref, out_ref):
    re, im = core_factor(unit_ref, False)
    half = mine_ref.shape[1]
    out_ref[pl.ds(0, half, 2), :] = re * mine_ref[0] - im * mine_ref[1]
    out_ref[pl.ds(1, half, 2), :] = re * mine_ref[1] + im * mine_ref[0]


def first_kernel(unit_ref, own_ref, other_ref, out_ref):
    re, im = core_factor(unit_ref, True)
    half = other_ref.shape[1]

    def store(_, carry):
        for c, add in (
            (0, re * other_ref[0] - im * other_ref[1]),
            (1, re * other_ref[1] + im * other_ref[0]),
        ):
            out_ref[pl.ds(c, half, 2), :] = own_ref[pl.ds(c, half, 2), :] + add
        return carry

    lax.fori_loop(0, 1 + REPEATS * core_of(), store, 0)


def middle_kernel(moved_ref, mid_ref, low_ref, out_ref):
    rows, order = moved_ref.shape
    size = rows // 4

    def place(pair, c):
        return pl.ds(pair * 2 + c, size, 4)

    stacked = jnp.concatenate(
        [
            jnp.concatenate([moved_ref[place(pair, c), :] for pair in range(2)], axis=1)
            for c in range(2)
        ],
        axis=0,
    )
    mixed = dot3((mid_ref[0], mid_ref[1]), split(stacked))
    turned = jnp.concatenate(
        [
            jnp.concatenate(
                [
                    mixed[c * size : (c + 1) * size, pair * order : (pair + 1) * order]
                    for c in range(2)
                ],
                axis=1,
            )
            for pair in range(2)
        ],
        axis=0,
    )
    last = dot3(split(turned), (low_ref[0], low_ref[1]))
    for pair in range(2):
        for c in range(2):
            out_ref[place(pair, c), :] = last[
                pair * size : (pair + 1) * size, c * order : (c + 1) * order
            ]


def last_kernel(rows_ref, out_ref):
    half = out_ref.shape[1]
    for c in range(2):
        out_ref[c] = rows_ref[pl.ds(c, half, 2), :]


def call(kernel, out, *operands):
    return pl.pallas_call(
        kernel,
        out_shape=out,
        in_specs=[IN_VMEM] * len(operands),
        out_specs=jax.tree.map(lambda _: IN_VMEM, out),
        compiler_params=pltpu.CompilerParams(vmem_limit_bytes=32 * 2**20),
    )(*operands)


def exchange(rows, stages, beside=()):
    blocks = rows.reshape(16, 64, -1)
    blocks = lax.all_to_all(blocks, AXIS, 0, 0, axis_index_groups=stages[0], tiled=True)
    blocks, beside = lax.optimization_barrier((blocks, beside))
    blocks = blocks.reshape(16, 16, 4, -1).transpose(1, 0, 2, 3).reshape(16, 64, -1)
    blocks = lax.all_to_all(blocks, AXIS, 0, 0, axis_index_groups=stages[1], tiled=True)
    return blocks.reshape(rows.shape), beside


def body(state, low_gates, low_order, high_gates, mid_gate, mid_order):
    order = state.shape[3]
    pairs = state.shape[1] * state.shape[2]
    rows = jax.ShapeDtypeStruct((2 * pairs, order), jnp.float32)

    mine = state.reshape(2, pairs, order)
    other = lax.ppermute(mine, AXIS, [(number, number ^ 128) for number in range(512)])
    units = jnp.broadcast_to(high_gates.reshape(16, 1), (16, order))
    own = call(own_kernel, rows, units, mine)
    sent = call(first_kernel, rows, units, own, other)
    sent, low_gates, low_order, mid_gate, mid_order = lax.optimization_barrier(
        (sent, low_gates, low_order, mid_gate, mid_order)
    )
    mid, low = call(
        gates_kernel,
        [
            jax.ShapeDtypeStruct((2, size * order, size * order), jnp.bfloat16)
            for size in (4, 2)
        ],
        low_order,
        mid_order.reshape(1, -1),
        units,
        low_gates,
        mid_gate,
    )
    moved, (mid, low) = exchange(sent, STAGES, (mid, low))
    done = call(middle_kernel, rows, moved, mid, low)
    back, _ = exchange(done, STAGES[::-1])
    final = jax.ShapeDtypeStruct(mine.shape, jnp.float32)
    return call(last_kernel, final, back).reshape(state.shape)


def solution(mesh):
    return jax.shard_map(
        body,
        mesh=Mesh(mesh.devices.reshape(-1), (AXIS,)),
        in_specs=(P(None, AXIS, None, None), P(), P(), P(), P(), P()),
        out_specs=P(None, AXIS, None, None),
        check_vma=False,
    )
```
